256 devices in a mesh: dp: 64 (over x, z_lo, y, core), mp: 4 (over z_hi).
Axes of the slice: x: 4, y: 4, z: 8 (z_hi: 4, z_lo: 2; z = z_hi * 2 + z_lo), core: 2. Of those that a mesh axis runs over, the one named last changes fastest.
Arguments:
- attn_out: bfloat16 [65536, 1024], P('dp'), may hold values from -16 to 16
- out_grad: bfloat16 [65536, 8192], P('dp', 'mp'), may hold values from -0.078125 to 0.078125
- left_old: float32 [1024, 1024], P('dp'), may hold values from -6 to 6
- right_old: float32 [4, 2048, 2048], P('mp', 'dp'), may hold values from -6 to 6
- basis: bfloat16 [4, 2048, 2048], P('mp', 'dp'), may hold values from -0.125 to 0.125
Outputs:
- left_new: float32 [1024, 1024], P('dp')
- right_new: float32 [4, 2048, 2048], P('mp', 'dp')
- rotated: bfloat16 [1024, 8192], P('dp', 'mp')
The draws below stay inside these ranges and needn't reach their ends.
All inputs are finite; a program needn't handle non-finite values.
Results may differ from the reference program's by a relative error of at most 0.003.
The reference program's roundings to bfloat16 on the way (of `grad_b`) count: a program that leaves them out, or rounds other values in their place, can miss the bound.
Values may be sent and summed in bfloat16 or wider, within the bound.
A program may use at most 64 MiB of HBM per device.

```python
import jax
import jax.numpy as jnp
from jax import lax

TOK_DEV = 1024
CB = 2048
TOKENS = 65536
WR = 1024
CT = 8192
N_DP = 64
N_MP = 4


def draw_out_grad(key, part):
    key = jax.random.fold_in(key, 11)
    values = jax.random.truncated_normal(key, -6.0, 6.0, (TOKENS, CT), jnp.float32)
    spread = 3.0
    blocks = CT // CB
    position = (jnp.arange(CT) // CB).astype(jnp.float32) / max(blocks - 1, 1)
    scale = spread ** (0.5 * position) / TOKENS ** 0.5
    return (values * scale[None, :]).astype(jnp.bfloat16)


def with_spikes(values, own_key, source, target, parts, factor):
    def block_of(dim):
        return (jnp.arange(values.shape[dim]) // (values.shape[dim] // parts)).reshape((-1,) + (1,) * (values.ndim - 1 - dim))

    one_side = jax.random.permutation(own_key, parts)[block_of(target)]
    far = (block_of(target) + parts // 2) % parts
    return jnp.where((block_of(source) == one_side) | (block_of(source) == far), factor * values, values)


def block_levels(own_key, extent, pieces, least, top_value):
    level, own = 1.0, jax.random.fold_in(own_key, 6)
    for dim, parts in pieces:
        steps = jnp.exp(jax.random.uniform(jax.random.fold_in(own, dim), (parts,), jnp.float32, least / len(pieces), top_value / len(pieces)))
        level = level * jnp.repeat(steps, extent[dim] // parts).reshape([-1 if axis == dim else 1 for axis in range(len(extent))])
    return level


def centred(own_key, dims, width, limit, pieces=(), held_as=jnp.bfloat16):
    result = width * jax.random.normal(own_key, dims, jnp.float32)
    if pieces:
        result = result * block_levels(own_key, dims, pieces, -0.22, 0.18)
    return jnp.clip(result, -limit, limit).astype(held_as)


def heavy_noise(rng, extent, scale, most, shards, heavy, dtype=jnp.bfloat16):
    array = scale * jax.random.normal(rng, extent, jnp.float32)
    if shards:
        array = array * block_levels(rng, extent, shards, -0.22, 0.18)
    return jnp.clip(with_spikes(array, jax.random.fold_in(rng, 3), *heavy), -most, most).astype(dtype)


def setup_inputs(seed: int = 0) -> dict:
    arg_keys = jax.random.split(jax.random.key(seed), 6)
    return {
        "attn_out": heavy_noise(arg_keys[0], (TOKENS, WR), 1.0, 16.0, ((0, 64),), (0, 1, 64, 4.0)),
        "out_grad": draw_out_grad(jax.random.fold_in(arg_keys[5], 71), 0),
        "left_old": centred(arg_keys[2], (WR, WR), 1.0, 6.0, ((0, 64),), jnp.float32),
        "right_old": centred(arg_keys[3], (N_MP, CB, CB), 1.0, 6.0, ((0, 4), (1, 64)), jnp.float32),
        "basis": centred(arg_keys[4], (N_MP, CB, CB), CB ** -0.5, 0.125, ((0, 4), (1, 64))),
    }


def reference(attn_out, out_grad, left_old, right_old, basis):
    xs = attn_out.reshape(N_DP, TOK_DEV, WR)
    gs = out_grad.reshape(N_DP, TOK_DEV, CT)

    def accumulate(total, pair):
        xblock, gblock = pair
        return total + jnp.dot(xblock.T, gblock, preferred_element_type=jnp.float32), None

    grad, _ = lax.scan(accumulate, jnp.zeros((WR, CT), jnp.float32), (xs, gs))
    grad_b = grad.astype(jnp.bfloat16)
    left_gram = jnp.dot(grad_b, grad_b.T, preferred_element_type=jnp.float32)
    left_new = 0.9 * left_old + 0.1 * (left_gram / CT)
    gf = grad_b.astype(jnp.float32).reshape(WR, N_MP, CB)
    right_gram = jnp.einsum("imk,iml->mkl", gf, gf)
    right_new = 0.9 * right_old + 0.1 * (right_gram / WR)
    rotated = jnp.einsum("imk,mkl->iml", gf, basis.astype(jnp.float32)).reshape(WR, CT)
    return left_new, right_new, rotated.astype(jnp.bfloat16)
```

```python
import functools

import jax
import jax.numpy as jnp
from jax import lax
from jax.experimental import pallas as pl
from jax.experimental.pallas import tpu as pltpu
from jax.sharding import PartitionSpec as P

MESH = pl.DeviceIdType.MESH
F32 = jnp.float32
BF16 = jnp.bfloat16

ROWS = 1024
TOK = 1024
COLS = 2048
HALF = 1024
W = 256
NC = HALF // W
N_SEM = 48 * NC + 48


def rows(start, size, unit=16):
    return pl.ds(pl.multiple_of(start, unit), size)


def kernel(
    a_hbm, g_hbm, left_hbm, right_hbm, basis_hbm,
    left_out, right_out, rot_out,
    a_v, at_v, g_v, p_v, pr_v, o_v, r1_v, t1_v, r2_v, t2_v, r3_v, cf_v,
    basis_v, bp_v, left_v, right_v, lacc_v, lr_v, ltot_v, racc_v, rsend_v, ct_v,
    ssem, rsem, lsem,
):
    dp = lax.axis_index("dp")
    mp = lax.axis_index("mp")
    x, z, y, c = dp // 16, (dp // 8) % 2, (dp // 2) % 4, dp % 2
    i1 = x * (1 - c) + y * c
    i2 = y * (1 - c) + x * c
    s1 = 16 * (1 - c) + 2 * c
    s2 = 2 * (1 - c) + 16 * c
    right1 = dp + ((i1 + 1) % 4 - i1) * s1
    left1 = dp + ((i1 + 3) % 4 - i1) * s1
    right2 = dp + ((i2 + 1) % 4 - i2) * s2
    left2 = dp + ((i2 + 3) % 4 - i2) * s2
    other_core = dp + 1 - 2 * c
    other_z = dp + (1 - 2 * z) * 8

    def plane(dx, dy):
        return ((x + dx) % 4) * 16 + z * 8 + ((y + dy) % 4) * 2 + c

    loads = {}

    def load(name, src, dst):
        copy = pltpu.make_async_copy(src, dst, lsem.at[len(loads)])
        copy.start()
        loads[name] = copy

    def a_load(r):
        load(("a", r), a_hbm.at[:, pl.ds(256 * r, 256)], a_v.at[r])

    def g_load(own, j):
        half = c if own else 1 - c
        load(
            ("g", own, j),
            g_hbm.at[:, pl.ds(pl.multiple_of(half * HALF + j * W, W), W)],
            g_v.at[j if own else NC + j],
        )

    a_load(0)
    g_load(False, 0)
    for r in range(1, 4):
        a_load(r)
    load("basis", basis_hbm.at[0], basis_v)
    g_load(True, 0)
    for j in range(1, NC):
        g_load(False, j)
        g_load(True, j)
    load("left", left_hbm, left_v)
    load("right", right_hbm.at[0], right_v)

    barrier = pltpu.get_barrier_semaphore()
    offsets = [(dx, dy) for dx in range(4) for dy in range(4) if (dx, dy) != (0, 0)]
    for dx, dy in offsets:
        pl.semaphore_signal(barrier, inc=1, device_id=(plane(dx, dy), mp), device_id_type=MESH)
    for device in (other_core, other_z):
        pl.semaphore_signal(barrier, inc=1, device_id=(device, mp), device_id_type=MESH)
    for d in range(1, 4):
        pl.semaphore_signal(barrier, inc=1, device_id=(dp, (mp + d) % 4), device_id_type=MESH)

    slots = {}
    started = []

    def slot(name):
        return slots.setdefault(name, len(slots))

    def send(name, src, dst, device, mp_to=None):
        n = slot(name)
        copy = pltpu.make_async_remote_copy(
            src_ref=src, dst_ref=dst, send_sem=ssem.at[n], recv_sem=rsem.at[n],
            device_id=(device, mp if mp_to is None else mp_to), device_id_type=MESH,
        )
        copy.start()
        started.append(copy)

    def recv(name, dst):
        n = slot(name)
        pltpu.make_async_remote_copy(
            src_ref=dst, dst_ref=dst, send_sem=ssem.at[n], recv_sem=rsem.at[n],
            device_id=(other_core, mp), device_id_type=MESH,
        ).wait_recv()

    def drain(count):
        for _ in range(min(count, len(started))):
            started.pop(0).wait_send()

    for r in range(4):
        loads[("a", r)].wait()
        at_v[256 * r:256 * (r + 1), :] = a_v[r].T

    pl.semaphore_wait(barrier, len(offsets) + 5)

    loads["basis"].wait()
    p_me = 4 * x + y
    zc = 2 * z + c

    def basis_slot(g, p):
        return bp_v.at[g, rows(p * 32, 32)]

    for dx, dy in offsets:
        p_to = 4 * ((x + dx) % 4) + (y + dy) % 4
        send(("basis", dx, dy), basis_v.at[:, rows(p_to * 128, 128, 128)], basis_slot(zc, p_me), plane(dx, dy))
    bp_v[zc, rows(p_me * 32, 32)] = basis_v[:, rows(p_me * 128, 128, 128)]

    def basis_gather():
        for dx, dy in offsets:
            p_from = 4 * ((x - dx + 4) % 4) + (y - dy + 4) % 4
            recv(("basis", dx, dy), basis_slot(zc, p_from))
        send("basis_core", bp_v.at[zc], bp_v.at[zc], other_core)
        send("basis_z", bp_v.at[zc], bp_v.at[zc], other_z)

    def basis_forward():
        from_z = 2 * (1 - z) + c
        recv("basis_z", bp_v.at[from_z])
        send("basis_fwd", bp_v.at[from_z], bp_v.at[from_z], other_core)

    def basis_end():
        recv("basis_core", bp_v.at[2 * z + 1 - c])
        recv("basis_fwd", bp_v.at[2 * (1 - z) + 1 - c])

    def compute(j):
        base = len(slots)
        for t in range(4):
            slot(("pair", j, t))
        loads[("g", False, j)].wait()

        def partner(t, carry):
            block = rows(((i2 + 6 - t) % 4) * 256, 256)
            p_v[j, block] = jnp.dot(at_v[block, :], g_v[NC + j], preferred_element_type=F32)
            pltpu.make_async_remote_copy(
                src_ref=p_v.at[j, block], dst_ref=pr_v.at[j, block],
                send_sem=ssem.at[base + t], recv_sem=rsem.at[base + t],
                device_id=(other_core, mp), device_id_type=MESH,
            ).start()
            return carry

        lax.fori_loop(0, 4, partner, 0)
        for t in range(4):
            block = rows(((i2 + 6 - t) % 4) * 256, 256)
            started.append(pltpu.make_async_remote_copy(
                src_ref=p_v.at[j, block], dst_ref=pr_v.at[j, block],
                send_sem=ssem.at[base + t], recv_sem=rsem.at[base + t],
                device_id=(other_core, mp), device_id_type=MESH,
            ))
        loads[("g", True, j)].wait()

        def own(t, carry):
            block = rows(((i1 + 6 - t) % 4) * 256, 256)
            o_v[j, block] = jnp.dot(at_v[block, :], g_v[j], preferred_element_type=F32)
            return carry

        lax.fori_loop(0, 4, own, 0)

    def pair_add(j, t):
        block = rows(((i1 + 6 - t) % 4) * 256, 256)
        recv(("pair", j, t), pr_v.at[j, block])
        o_v[j, block] += pr_v[j, block]

    def ring(tag, src, land, unit, i, to_right, to_left):
        h = unit // 2

        def part(q, half):
            return rows((q % 4) * unit + half * h, h)

        def far():
            send((tag, 0), src.at[part(i + 2, 0)], land.at[0], to_right)
            send((tag, 1), src.at[part(i + 2, 1)], land.at[1], to_left)

        def direct_right():
            send((tag, 2), src.at[part(i + 1, 1)], land.at[2], to_right)

        def direct_left():
            send((tag, 3), src.at[part(i + 3, 0)], land.at[3], to_left)

        def aggregate():
            recv((tag, 0), land.at[0])
            src[part(i + 1, 0), :] += land[0]
            send((tag, 4), src.at[part(i + 1, 0)], land.at[4], to_right)
            recv((tag, 1), land.at[1])
            src[part(i + 3, 1), :] += land[1]
            send((tag, 5), src.at[part(i + 3, 1)], land.at[5], to_left)

        def finish(dst):
            recv((tag, 2), land.at[2])
            recv((tag, 3), land.at[3])
            recv((tag, 4), land.at[4])
            dst[0:h, :] = src[part(i, 0), :] + land[3] + land[4]
            recv((tag, 5), land.at[5])
            dst[h:unit, :] = src[part(i, 1), :] + land[2] + land[5]

        return far, direct_right, direct_left, aggregate, finish

    def gather(tag, buf, base, unit, i, to_right, to_left):
        h = unit // 2

        def part(q, half, size):
            return rows(base + (q % 4) * unit + half * h, size)

        def begin():
            own = buf.at[part(i, 0, unit)]
            send((tag, 0), own, own, to_right)
            send((tag, 1), own, own, to_left)

        def forward():
            recv((tag, 0), buf.at[part(i + 3, 0, unit)])
            half = buf.at[part(i + 3, 0, h)]
            send((tag, 2), half, half, to_right)
            recv((tag, 1), buf.at[part(i + 1, 0, unit)])
            half = buf.at[part(i + 1, 1, h)]
            send((tag, 3), half, half, to_left)

        def end():
            recv((tag, 2), buf.at[part(i + 2, 0, h)])
            recv((tag, 3), buf.at[part(i + 2, 1, h)])

        return begin, forward, end

    lacc_v[...] = jnp.zeros_like(lacc_v)
    racc_v[...] = jnp.zeros_like(racc_v)

    def chunk(j):
        k = NC * c + j
        k_other = NC * (1 - c) + j
        buf = cf_v.at[k]
        ring1 = ring(("r1", j), o_v.at[j], r1_v.at[j], 256, i1, right1, left1)
        ring2 = ring(("r2", j), t1_v.at[j], r2_v.at[j], 64, i2, right2, left2)
        gather2 = gather(("g2", j), buf, i1 * 256, 64, i2, right2, left2)
        gather1 = gather(("g1", j), buf, 0, 256, i1, right1, left1)
        row0 = i1 * 256 + i2 * 64

        def to_core(q, n):
            block = buf.at[rows((q % 4) * 256, 256)]
            send(("core", j, n), block, block, other_core)

        def act0():
            compute(j)

        def act1():
            pair_add(j, 0)
            ring1[0]()
            pair_add(j, 1)
            ring1[1]()
            pair_add(j, 3)
            ring1[2]()
            pair_add(j, 2)

        def act2():
            ring1[3]()

        def act3():
            ring1[4](t1_v.at[j])
            ring2[0]()
            ring2[1]()
            ring2[2]()

        def act4():
            ring2[3]()

        def act5():
            ring2[4](t2_v.at[j])
            send(("z", j), t2_v.at[j, rows((1 - z) * 32, 32)], r3_v.at[j], other_z)

        def act6():
            recv(("z", j), r3_v.at[j])
            mine = buf.at[rows(row0 + z * 32, 32)]
            mine[...] = (t2_v[j, rows(z * 32, 32)] + r3_v[j]).astype(BF16)
            send(("gz", j), mine, mine, other_z)

        def act7():
            recv(("gz", j), buf.at[rows(row0 + (1 - z) * 32, 32)])
            gather2[0]()

        def act8():
            gather2[1]()

        def act9():
            gather2[2]()
            gather1[0]()
            to_core(i1, 0)

        def act10():
            gather1[1]()
            to_core(i1 + 3, 1)
            to_core(i1 + 1, 2)

        def act11():
            gather1[2]()
            to_core(i1 + 2, 3)

        def act12():
            other = cf_v.at[k_other]
            for n, q in enumerate((i2, i2 + 3, i2 + 1, i2 + 2)):
                recv(("core", j, n), other.at[rows((q % 4) * 256, 256)])

        def act13():
            def one(n, carry):
                kk = NC * n + j
                lacc_v[...] += lax.dot_general(
                    cf_v[kk, rows(dp * 16, 16)], cf_v[kk], (((1,), (1,)), ((), ())),
                    preferred_element_type=F32,
                )
                lhs = jnp.concatenate(
                    [cf_v[kk, rows(256 * xx + 128 * z + 32 * yy + 16 * c, 16)] for xx in range(4) for yy in range(4)], 0
                )
                rhs = jnp.concatenate(
                    [bp_v[2 * (kk % 2) + cc, rows((4 * (kk // 2) + yy) * 32, 32)] for yy in range(4) for cc in range(2)], 0
                )
                racc_v[...] += jnp.dot(lhs, rhs, preferred_element_type=F32)
                return carry

            lax.fori_loop(0, 2, one, 0)

        return (act0, act1, act2, act3, act4, act5, act6, act7, act8, act9, act10, act11, act12, act13)

    chunks = [chunk(j) for j in range(NC)]
    period, start = 4.0, (0.0, 1.5, 3.5, 6.0, 7.5, 9.0, 10.5, 12.0, 13.5, 15.0, 17.0, 19.0, 20.5, 21.0)
    order = sorted((j * period + start[s], s, j) for j in range(NC) for s in range(len(start)))
    marks = {(0, 1): basis_gather, (0, 2): basis_forward, (0, 5): basis_end}
    for _, s, j in order:
        if (j, s) in marks:
            marks[(j, s)]()
        chunks[j][s]()
        if s >= 7:
            drain(8)

    def quarter(ref, m):
        return ref.at[:, rows((m % 4) * 256, 256, 256)]

    for d in range(1, 4):
        send(("ls", d), quarter(lacc_v, mp + d), lr_v.at[d], dp, (mp + d) % 4)

    rsend_v[...] = racc_v[...].astype(BF16)
    mine = rows(p_me * 128, 128, 128)
    for dx, dy in offsets:
        p_to = 4 * ((x + dx) % 4) + (y + dy) % 4
        send(("rot", dx, dy), rsend_v.at[rows(p_to * 16, 16)], rot_out.at[:, mine], plane(dx, dy))
    rot_out[:, mine] = rsend_v[rows(p_me * 16, 16), :]

    group = rows(128 * ((dp // 4) % 2), 128, 128)
    ct_v[...] = cf_v[dp // 8, :, group].T
    loads["right"].wait()

    def right_step(k, carry):
        cols = rows(k * 256, 256, 256)
        gram = jnp.dot(ct_v[rows(32 * (dp % 4), 32), :], cf_v[k], preferred_element_type=F32)
        right_out[0, :, cols] = 0.9 * right_v[:, cols] + 0.1 * (gram / ROWS)
        return carry

    lax.fori_loop(0, 4, right_step, 0)

    for d in range(1, 4):
        recv(("ls", d), lr_v.at[d])
    my_quarter = rows(mp * 256, 256, 256)
    ltot_v[:, my_quarter] = lacc_v[:, my_quarter] + lr_v[1] + lr_v[2] + lr_v[3]
    for d in range(1, 4):
        send(("lg", d), quarter(ltot_v, mp), quarter(ltot_v, mp), dp, (mp + d) % 4)

    lax.fori_loop(4, 8, right_step, 0)

    loads["left"].wait()
    for d in range(1, 4):
        recv(("lg", d), quarter(ltot_v, mp + 4 - d))
    left_out[...] = 0.9 * left_v[...] + 0.1 * (ltot_v[...] / (4 * COLS))
    for dx, dy in offsets:
        p_from = 4 * ((x - dx + 4) % 4) + (y - dy + 4) % 4
        recv(("rot", dx, dy), rot_out.at[:, rows(p_from * 128, 128, 128)])
    drain(len(started))


def body(attn_out, out_grad, left_old, right_old, basis):
    vmem = pl.BlockSpec(memory_space=pltpu.VMEM)
    hbm = pl.BlockSpec(memory_space=pl.ANY)
    v = pltpu.VMEM
    return pl.pallas_call(
        kernel,
        out_shape=(
            jax.ShapeDtypeStruct((16, ROWS), F32),
            jax.ShapeDtypeStruct((1, 32, COLS), F32),
            jax.ShapeDtypeStruct((16, COLS), BF16),
        ),
        in_specs=[hbm] * 5,
        out_specs=(vmem, vmem, vmem),
        scratch_shapes=[
            v((4, TOK, 256), BF16),
            v((ROWS, TOK), BF16),
            v((2 * NC, TOK, W), BF16),
            v((NC, ROWS, W), F32),
            v((NC, ROWS, W), F32),
            v((NC, ROWS, W), F32),
            v((NC, 6, 128, W), F32),
            v((NC, 256, W), F32),
            v((NC, 6, 32, W), F32),
            v((NC, 64, W), F32),
            v((NC, 32, W), F32),
            v((2 * NC, ROWS, W), BF16),
            v((32, COLS), BF16),
            v((4, 512, 128), BF16),
            v((16, ROWS), F32),
            v((32, COLS), F32),
            v((16, ROWS), F32),
            v((4, 16, 256), F32),
            v((16, ROWS), F32),
            v((256, 128), F32),
            v((256, 128), BF16),
            v((128, ROWS), BF16),
            pltpu.SemaphoreType.DMA((N_SEM,)),
            pltpu.SemaphoreType.DMA((N_SEM,)),
            pltpu.SemaphoreType.DMA((8 + 2 * NC,)),
        ],
        compiler_params=pltpu.CompilerParams(
            collective_id=0, has_side_effects=True, vmem_limit_bytes=52 * 1024 * 1024,
        ),
        cost_estimate=pl.CostEstimate(flops=5 * 10**9, bytes_accessed=7 * 2**20, transcendentals=0),
    )(attn_out, out_grad, left_old, right_old, basis)


def solution(mesh):
    return jax.shard_map(
        body,
        mesh=mesh,
        in_specs=(
            P("dp", None),
            P("dp", "mp"),
            P("dp", None),
            P("mp", "dp", None),
            P("mp", "dp", None),
        ),
        out_specs=(P("dp", None), P("mp", "dp", None), P("dp", "mp")),
        check_vma=False,
    )
```

```python
import jax
import jax.numpy as jnp
from jax import lax
from jax.experimental import pallas as pl
from jax.experimental.pallas import tpu as pltpu
from jax.sharding import PartitionSpec as P

MESH = pl.DeviceIdType.MESH
F32 = jnp.float32
BF16 = jnp.bfloat16

ROWS = 1024
TOK = 1024
COLS = 2048
HALF = 1024
W = 256
NC = HALF // W

PLANE = [(dx, dy) for dx in range(4) for dy in range(4) if (dx, dy) != (0, 0)]
EIGHT = [(di, dz) for di in range(4) for dz in range(2) if (di, dz) != (0, 0)]

ORDER = [
    ("partner", 1), ("own", 0), ("partner", 2), ("own", 1), ("far", 0), ("partner", 3), ("own", 2),
    ("direct", 0), ("far", 1), ("own", 3), ("aggregate", 0), ("direct", 1), ("far", 2), ("direct", 2),
    ("far", 3), ("aggregate", 1), ("direct", 3), ("finish", 0), ("aggregate", 2), ("aggregate", 3),
    ("finish", 1), ("total", 0), ("basis_gather", 0), ("finish", 2), ("finish", 3), ("total", 1), ("gather", 0),
    ("total", 2), ("total", 3), ("basis_forward", 0), ("forward", 0), ("gather", 1), ("gather", 2), ("end", 0),
    ("gather", 3), ("basis_end", 0), ("products", 0), ("forward", 1), ("forward", 2), ("forward", 3), ("end", 1),
    ("end", 2), ("products", 1), ("end", 3), ("products", 2), ("products", 3),
]


def rows(start, size, unit=16):
    return pl.ds(pl.multiple_of(start, unit), size)


def kernel(
    a_hbm, g_hbm, left_hbm, right_hbm, basis_hbm,
    left_out, right_out, rot_out,
    a_v, g_v, p_v, pr_v, o_v, r1_v, t1_v, r2_v, cf_v,
    basis_v, bp_v, left_v, right_v, lacc_v, lr_v, racc_v, rsend_v, ct_v,
    ssem, rsem, lsem,
):
    dp = lax.axis_index("dp")
    mp = lax.axis_index("mp")
    x, z, y, c = dp // 16, (dp // 8) % 2, (dp // 2) % 4, dp % 2
    i1 = x * (1 - c) + y * c
    i2 = y * (1 - c) + x * c
    s1 = 16 * (1 - c) + 2 * c
    s2 = 2 * (1 - c) + 16 * c
    right1 = dp + ((i1 + 1) % 4 - i1) * s1
    left1 = dp + ((i1 + 3) % 4 - i1) * s1
    other_core = dp + 1 - 2 * c
    other_z = dp + (1 - 2 * z) * 8

    def plane(dx, dy):
        return ((x + dx) % 4) * 16 + z * 8 + ((y + dy) % 4) * 2 + c

    def eight(di, dz):
        return dp + ((i2 + di) % 4 - i2) * s2 + ((z + dz) % 2 - z) * 8

    barrier = pltpu.get_barrier_semaphore()
    greeted = [(plane(dx, dy), mp) for dx, dy in PLANE] + [(eight(di, 1), mp) for di in range(4)]
    greeted += [(other_core, mp)] + [(dp, (mp + d) % 4) for d in range(1, 4)]
    for device in greeted:
        pl.semaphore_signal(barrier, inc=1, device_id=device, device_id_type=MESH)

    loads = {}

    def load(name, src, dst):
        copy = pltpu.make_async_copy(src, dst, lsem.at[len(loads)])
        copy.start()
        loads[name] = copy

    def g_load(own, j):
        half = c if own else 1 - c
        load(
            ("g", own, j),
            g_hbm.at[:, rows(half * HALF + j * W, W, W)],
            g_v.at[j if own else NC + j],
        )

    load("a", a_hbm, a_v)
    g_load(False, 0)
    g_load(True, 0)
    load("basis", basis_hbm.at[0], basis_v)
    for j in range(1, NC):
        g_load(False, j)
        g_load(True, j)
    load("left", left_hbm, left_v)
    load("right", right_hbm.at[0], right_v)

    sent, landed = {}, {}

    def descriptor(src, dst, out, into, device):
        return pltpu.make_async_remote_copy(
            src_ref=src, dst_ref=dst,
            send_sem=ssem.at[sent.setdefault(out, len(sent))],
            recv_sem=rsem.at[landed.setdefault(into, len(landed))],
            device_id=device, device_id_type=MESH,
        )

    def send(src, dst, out, into, device):
        descriptor(src, dst, out, into, device).start()

    def recv(into, span):
        pltpu.make_async_copy(span, span, rsem.at[landed[into]]).wait()

    def wait_sent(out, span):
        pltpu.make_async_copy(span, span, ssem.at[sent[out]]).wait()

    p_me = 4 * x + y
    zc = 2 * z + c

    def basis_begin():
        loads["basis"].wait()
        for dx, dy in PLANE:
            p_to = 4 * ((x + dx) % 4) + (y + dy) % 4
            send(
                basis_v.at[:, rows(p_to * 128, 128, 128)], bp_v.at[zc, rows(p_me * 32, 32)],
                "basis", "basis", (plane(dx, dy), mp),
            )
        bp_v[zc, rows(p_me * 32, 32)] = basis_v[:, rows(p_me * 128, 128, 128)]

    def basis_gather():
        recv("basis", bp_v.at[zc, 0:480])
        send(bp_v.at[zc], bp_v.at[zc], "basis_core", "basis_core", (other_core, mp))
        send(bp_v.at[zc], bp_v.at[zc], "basis_z", "basis_z", (other_z, mp))

    def basis_forward():
        from_z = 2 * (1 - z) + c
        recv("basis_z", bp_v.at[from_z])
        send(bp_v.at[from_z], bp_v.at[from_z], "basis_forward", "basis_forward", (other_core, mp))

    def basis_end():
        recv("basis_core", bp_v.at[2 * z + 1 - c])
        recv("basis_forward", bp_v.at[2 * (1 - z) + 1 - c])

    def quarter1(i):
        return (i % 4) * 256

    def partner_product(j):
        loads[("g", False, j)].wait()
        p_v[j] = lax.dot_general(a_v[...], g_v[NC + j], (((0,), (0,)), ((), ())), preferred_element_type=F32)

    def partner_send(j):
        if j == 0:
            for t in (2, 1, 3, 0):
                block = rows(quarter1(i2 + t), 256)
                send(p_v.at[j, block], pr_v.at[j, block], "pair", ("pair", j, t), (other_core, mp))
        else:
            send(p_v.at[j], pr_v.at[j], "pair", ("pair", j), (other_core, mp))

    def partner(j):
        partner_product(j)
        partner_send(j)

    def own(j):
        loads[("g", True, j)].wait()
        o_v[j] = lax.dot_general(a_v[...], g_v[j], (((0,), (0,)), ((), ())), preferred_element_type=F32)

    def part(i, half):
        return rows(quarter1(i) + half * 128, 128)

    def far(j):
        for t in (2, 1, 3, 0):
            block = rows(quarter1(i1 + t), 256)
            if j == 0:
                recv(("pair", j, t), pr_v.at[j, block])
            elif t == 2:
                recv(("pair", j), pr_v.at[j])
            o_v[j, block] += pr_v[j, block]
            if t == 2:
                src, land = o_v.at[j], r1_v.at[j]
                send(src.at[part(i1 + 2, 0)], land.at[0], "ring", ("far", j), (right1, mp))
                send(src.at[part(i1 + 2, 1)], land.at[1], "ring", ("far", j), (left1, mp))

    def direct(j):
        src, land = o_v.at[j], r1_v.at[j]
        send(src.at[part(i1 + 1, 1)], land.at[2], "ring", ("near", j), (right1, mp))
        send(src.at[part(i1 + 3, 0)], land.at[3], "ring", ("near", j), (left1, mp))

    def aggregate(j):
        src, land = o_v.at[j], r1_v.at[j]
        recv(("far", j), land.at[0:2])
        src[part(i1 + 1, 0), :] += land[0]
        send(src.at[part(i1 + 1, 0)], land.at[4], "ring", ("near", j), (right1, mp))
        src[part(i1 + 3, 1), :] += land[1]
        send(src.at[part(i1 + 3, 1)], land.at[5], "ring", ("near", j), (left1, mp))

    def finish(j):
        src, land, dst = o_v.at[j], r1_v.at[j], t1_v.at[j]
        recv(("near", j), land.at[2:6])
        dst[0:128, :] = src[part(i1, 0), :] + land[3] + land[4]
        dst[128:256, :] = src[part(i1, 1), :] + land[2] + land[5]
        for n, (di, dz) in enumerate(EIGHT):
            block = rows(((i2 + di) % 4) * 64 + ((z + dz) % 2) * 32, 32)
            send(dst.at[block], r2_v.at[j, n], "eight", ("eight", j), (eight(di, dz), mp))

    def total(j):
        recv(("eight", j), r2_v.at[j])
        value = t1_v[j, rows(i2 * 64 + z * 32, 32)]
        for n in range(len(EIGHT)):
            value += r2_v[j, n]
        mine = cf_v.at[NC * c + j, rows(i1 * 256 + i2 * 64 + z * 32, 32)]
        mine[...] = value.astype(BF16)
        for di, dz in EIGHT:
            send(mine, mine, ("all8", j), ("all8", j), (eight(di, dz), mp))

    def to_core(j, i):
        block = cf_v.at[NC * c + j, rows(quarter1(i), 256)]
        send(block, block, ("core", j), ("core", j), (other_core, mp))

    def gather(j):
        buf = cf_v.at[NC * c + j]
        recv(("all8", j), buf.at[rows(quarter1(i1), 224)])
        block = buf.at[rows(quarter1(i1), 256)]
        send(block, block, ("ring8", j), ("begin", j), (right1, mp))
        send(block, block, ("ring8", j), ("begin", j), (left1, mp))
        to_core(j, i1)

    def forward(j):
        buf = cf_v.at[NC * c + j]
        recv(("begin", j), buf.at[0:512])
        half = buf.at[part(i1 + 3, 0)]
        send(half, half, ("ring8", j), ("forward", j), (right1, mp))
        half = buf.at[part(i1 + 1, 1)]
        send(half, half, ("ring8", j), ("forward", j), (left1, mp))
        to_core(j, i1 + 3)
        to_core(j, i1 + 1)

    def end(j):
        recv(("forward", j), cf_v.at[NC * c + j, 0:256])
        to_core(j, i1 + 2)

    def products(j):
        recv(("core", j), cf_v.at[NC * (1 - c) + j])

        def one(n, carry):
            k = NC * n + j
            lacc_v[...] += lax.dot_general(
                cf_v[k, rows(dp * 16, 16)], cf_v[k], (((1,), (1,)), ((), ())), preferred_element_type=F32
            )
            lhs = jnp.concatenate(
                [cf_v[k, rows(256 * xx + 128 * z + 32 * yy + 16 * c, 16)] for xx in range(4) for yy in range(4)], 0
            )
            rhs = jnp.concatenate(
                [bp_v[2 * (k % 2) + cc, rows((4 * (k // 2) + yy) * 32, 32)] for yy in range(4) for cc in range(2)], 0
            )
            racc_v[...] += jnp.dot(lhs, rhs, preferred_element_type=F32)
            return carry

        lax.fori_loop(0, 2, one, 0)

    steps = {
        "partner": partner, "own": own, "far": far, "direct": direct, "aggregate": aggregate, "finish": finish,
        "total": total, "gather": gather, "forward": forward, "end": end, "products": products,
        "basis_gather": lambda j: basis_gather(), "basis_forward": lambda j: basis_forward(),
        "basis_end": lambda j: basis_end(),
    }

    loads["a"].wait()
    with jax.named_scope("first"):
        partner_product(0)
        lacc_v[...] = jnp.zeros_like(lacc_v)
        racc_v[...] = jnp.zeros_like(racc_v)
    with jax.named_scope("barrier"):
        pl.semaphore_wait(barrier, len(greeted))
    partner_send(0)
    basis_begin()
    for step, j in ORDER:
        with jax.named_scope(f"{step}_{j}"):
            steps[step](j)

    with jax.named_scope("left_send"):
        lr_v[mp] = lacc_v[...].astype(BF16)
        for d in range(1, 4):
            send(lr_v.at[mp], lr_v.at[mp], "left", "left", (dp, (mp + d) % 4))

    with jax.named_scope("rotated_send"):
        rsend_v[...] = racc_v[...].astype(BF16)
        mine = rows(p_me * 128, 128, 128)
        for dx, dy in PLANE:
            p_to = 4 * ((x + dx) % 4) + (y + dy) % 4
            send(rsend_v.at[rows(p_to * 16, 16)], rot_out.at[:, mine], "rotated", "rotated", (plane(dx, dy), mp))
        rot_out[:, mine] = rsend_v[rows(p_me * 16, 16), :]

    with jax.named_scope("right"):
        ct_v[...] = cf_v[dp // 8, :, rows(128 * ((dp // 4) % 2), 128, 128)].T
        loads["right"].wait()

        def right_step(k, carry):
            cols = rows(k * 256, 256, 256)
            gram = jnp.dot(ct_v[rows(32 * (dp % 4), 32), :], cf_v[k], preferred_element_type=F32)
            right_out[0, :, cols] = 0.9 * right_v[:, cols] + 0.1 * (gram / ROWS)
            return carry

        lax.fori_loop(0, 2 * NC, right_step, 0)

    with jax.named_scope("sent"):
        wait_sent("pair", p_v)
        wait_sent("ring", r1_v)
        wait_sent("eight", r2_v)
        for j in range(NC):
            wait_sent(("all8", j), cf_v.at[0, 0:224])
            wait_sent(("ring8", j), cf_v.at[0, 0:768])
            wait_sent(("core", j), cf_v.at[0])
        wait_sent("basis", bp_v.at[0, 0:480])
        for name in ("basis_core", "basis_z", "basis_forward"):
            wait_sent(name, bp_v.at[0])
        wait_sent("rotated", rsend_v.at[0:240])
        wait_sent("left", lr_v.at[0:3])
    with jax.named_scope("rotated_recv"):
        recv("rotated", rsend_v.at[0:240])
    with jax.named_scope("left_recv"):
        loads["left"].wait()
        recv("left", lr_v.at[0:3])
        gram = lr_v[0].astype(F32) + lr_v[1].astype(F32) + lr_v[2].astype(F32) + lr_v[3].astype(F32)
        left_out[...] = 0.9 * left_v[...] + 0.1 * (gram / (4 * COLS))


def body(attn_out, out_grad, left_old, right_old, basis):
    vmem = pl.BlockSpec(memory_space=pltpu.VMEM)
    hbm = pl.BlockSpec(memory_space=pltpu.HBM)
    v = pltpu.VMEM
    args = [pltpu.with_memory_space_constraint(a, pltpu.HBM) for a in (attn_out, out_grad, left_old, right_old, basis)]
    return pl.pallas_call(
        kernel,
        out_shape=(
            jax.ShapeDtypeStruct((16, ROWS), F32),
            jax.ShapeDtypeStruct((1, 32, COLS), F32),
            jax.ShapeDtypeStruct((16, COLS), BF16),
        ),
        in_specs=[hbm] * 5,
        out_specs=(vmem, vmem, vmem),
        scratch_shapes=[
            v((TOK, ROWS), BF16),
            v((2 * NC, TOK, W), BF16),
            v((NC, ROWS, W), F32),
            v((NC, ROWS, W), F32),
            v((NC, ROWS, W), F32),
            v((NC, 6, 128, W), F32),
            v((NC, 256, W), F32),
            v((NC, 7, 32, W), F32),
            v((2 * NC, ROWS, W), BF16),
            v((32, COLS), BF16),
            v((4, 512, 128), BF16),
            v((16, ROWS), F32),
            v((32, COLS), F32),
            v((16, ROWS), F32),
            v((4, 16, ROWS), BF16),
            v((256, 128), F32),
            v((256, 128), BF16),
            v((128, ROWS), BF16),
            pltpu.SemaphoreType.DMA((24,)),
            pltpu.SemaphoreType.DMA((44,)),
            pltpu.SemaphoreType.DMA((12,)),
        ],
        compiler_params=pltpu.CompilerParams(
            collective_id=0, has_side_effects=True, vmem_limit_bytes=48 * 1024 * 1024,
        ),
        cost_estimate=pl.CostEstimate(flops=5 * 10**9, bytes_accessed=7 * 2**20, transcendentals=0),
    )(*args)


def solution(mesh):
    return jax.shard_map(
        body,
        mesh=mesh,
        in_specs=(
            P("dp", None),
            P("dp", "mp"),
            P("dp", None),
            P("mp", "dp", None),
            P("mp", "dp", None),
        ),
        out_specs=(P("dp", None), P("mp", "dp", None), P("dp", "mp")),
        check_vma=False,
    )
```

```python
import jax
import jax.numpy as jnp
from jax import lax
from jax.experimental import pallas as pl
from jax.experimental.pallas import tpu as pltpu
from jax.sharding import PartitionSpec as P

MESH = pl.DeviceIdType.MESH
F32 = jnp.float32
BF16 = jnp.bfloat16

ROWS = 1024
TOK = 1024
COLS = 2048
HALF = 1024
W = 256
NC = HALF // W

PLANE = [(dx, dy) for dx in range(4) for dy in range(4) if (dx, dy) != (0, 0)]
EIGHT = [(di, dz) for di in range(4) for dz in range(2) if (di, dz) != (0, 0)]

ORDER = [
    ("partner", 1), ("own", 1), ("partner", 2), ("aggregate", 0), ("far", 1), ("own", 2), ("direct", 1), ("far", 2),
    ("finish", 0), ("basis_gather", 0), ("partner", 3), ("aggregate", 1), ("own", 3), ("direct", 2), ("aggregate", 2),
    ("far", 3), ("total", 0), ("finish", 1), ("direct", 3), ("aggregate", 3), ("basis_forward", 0), ("finish", 2),
    ("total", 1), ("gather", 0), ("finish", 3), ("total", 2), ("gather", 1), ("total", 3), ("gather", 2),
    ("gather", 3), ("basis_end", 0), ("end", 0), ("end", 1), ("end", 2), ("end", 3), ("products", 0), ("products", 1),
    ("products", 2), ("products", 3),
]


def rows(start, size, unit=16):
    return pl.ds(pl.multiple_of(start, unit), size)


def kernel(
    a_hbm, g_hbm, left_hbm, right_hbm, basis_hbm,
    left_out, right_out, rot_out,
    a_v, g_v, p_v, pr_v, o_v, r1_v, t1_v, r2_v, cf_v,
    basis_v, bp_v, left_v, right_v, lacc_v, lr_v, racc_v, rsend_v, ct_v,
    ssem, rsem, lsem,
):
    dp = lax.axis_index("dp")
    mp = lax.axis_index("mp")
    x, z, y, c = dp // 16, (dp // 8) % 2, (dp // 2) % 4, dp % 2
    i1 = x * (1 - c) + y * c
    i2 = y * (1 - c) + x * c
    s1 = 16 * (1 - c) + 2 * c
    s2 = 2 * (1 - c) + 16 * c
    right1 = dp + ((i1 + 1) % 4 - i1) * s1
    left1 = dp + ((i1 + 3) % 4 - i1) * s1
    opposite1 = dp + ((i1 + 2) % 4 - i1) * s1
    other_core = dp + 1 - 2 * c
    other_z = dp + (1 - 2 * z) * 8

    def plane(dx, dy):
        return ((x + dx) % 4) * 16 + z * 8 + ((y + dy) % 4) * 2 + c

    def eight(di, dz):
        return dp + ((i2 + di) % 4 - i2) * s2 + ((z + dz) % 2 - z) * 8

    barrier = pltpu.get_barrier_semaphore()
    greeted = [(plane(dx, dy), mp) for dx, dy in PLANE] + [(eight(di, 1), mp) for di in range(4)]
    greeted += [(other_core, mp)] + [(dp, (mp + d) % 4) for d in range(1, 4)]
    for device in greeted:
        pl.semaphore_signal(barrier, inc=1, device_id=device, device_id_type=MESH)

    loads = {}

    def load(name, src, dst):
        copy = pltpu.make_async_copy(src, dst, lsem.at[len(loads)])
        copy.start()
        loads[name] = copy

    def g_load(own, j):
        half = c if own else 1 - c
        load(
            ("g", own, j),
            g_hbm.at[:, rows(half * HALF + j * W, W, W)],
            g_v.at[j if own else NC + j],
        )

    def a_load(n):
        cols = rows(((first_half + n) % 2) * 512, 512, 512)
        load(("a", n), a_hbm.at[:, cols], a_v.at[:, cols])

    first_half = ((i2 + 2) % 4) // 2
    a_load(0)
    g_load(False, 0)
    a_load(1)
    g_load(True, 0)
    load("basis", basis_hbm.at[0], basis_v)

    def later_loads():
        for j in range(1, NC):
            g_load(False, j)
            g_load(True, j)
        load("left", left_hbm, left_v)
        load("right", right_hbm.at[0], right_v)

    sent, landed = {}, {}

    def descriptor(src, dst, out, into, device):
        return pltpu.make_async_remote_copy(
            src_ref=src, dst_ref=dst,
            send_sem=ssem.at[sent.setdefault(out, len(sent))],
            recv_sem=rsem.at[landed.setdefault(into, len(landed))],
            device_id=device, device_id_type=MESH,
        )

    def send(src, dst, out, into, device):
        descriptor(src, dst, out, into, device).start()

    def recv(into, span):
        pltpu.make_async_copy(span, span, rsem.at[landed[into]]).wait()

    def wait_sent(out, span):
        pltpu.make_async_copy(span, span, ssem.at[sent[out]]).wait()

    p_me = 4 * x + y
    zc = 2 * z + c

    def basis_begin():
        loads["basis"].wait()
        for dx, dy in PLANE:
            p_to = 4 * ((x + dx) % 4) + (y + dy) % 4
            send(
                basis_v.at[:, rows(p_to * 128, 128, 128)], bp_v.at[zc, rows(p_me * 32, 32)],
                "basis", "basis", (plane(dx, dy), mp),
            )
        bp_v[zc, rows(p_me * 32, 32)] = basis_v[:, rows(p_me * 128, 128, 128)]

    def basis_gather():
        recv("basis", bp_v.at[zc, 0:480])
        send(bp_v.at[zc], bp_v.at[zc], "basis_core", "basis_core", (other_core, mp))
        send(bp_v.at[zc], bp_v.at[zc], "basis_z", "basis_z", (other_z, mp))

    def basis_forward():
        from_z = 2 * (1 - z) + c
        recv("basis_z", bp_v.at[from_z])
        send(bp_v.at[from_z], bp_v.at[from_z], "basis_forward", "basis_forward", (other_core, mp))

    def basis_end():
        recv("basis_core", bp_v.at[2 * z + 1 - c])
        recv("basis_forward", bp_v.at[2 * (1 - z) + 1 - c])

    def quarter1(i):
        return (i % 4) * 256

    def product(dst, g, half):
        block = rows(half * 512, 512, 512)
        dst[block, :] = lax.dot_general(
            a_v[:, block], g[...], (((0,), (0,)), ((), ())), preferred_element_type=F32
        )

    def both_halves(dst, g):
        def one(half, carry):
            product(dst, g, half)
            return carry

        lax.fori_loop(0, 2, one, 0)

    def partner(j):
        loads[("g", False, j)].wait()
        both_halves(p_v.at[j], g_v.at[NC + j])
        send(p_v.at[j], pr_v.at[j], "pair", ("pair", j), (other_core, mp))

    def own(j):
        loads[("g", True, j)].wait()
        both_halves(o_v.at[j], g_v.at[j])

    def first_chunk():
        p, o = p_v.at[0], o_v.at[0]
        my_half = ((i1 + 2) % 4) // 2
        for n in range(2):
            half = (first_half + n) % 2
            loads[("a", n)].wait()
            if n == 0:
                loads[("g", False, 0)].wait()
            with jax.named_scope("first"):
                product(p, g_v.at[NC], half)
            if n == 0:
                with jax.named_scope("barrier"):
                    pl.semaphore_wait(barrier, len(greeted))
            block = rows(half * 512, 512, 512)
            send(p.at[block], pr_v.at[0, block], "pair", ("pair", 0, n), (other_core, mp))
        basis_begin()
        later_loads()
        loads[("g", True, 0)].wait()
        for n in range(2):
            half = (my_half + n) % 2
            with jax.named_scope("first"):
                product(o, g_v.at[0], half)
            block = rows(half * 512, 512, 512)
            recv(("pair", 0, n), pr_v.at[0, block])
            o[block, :] += pr_v[0, block]
            if n == 0:
                send_far(0)
        direct(0)

    def part(i, half):
        return rows(quarter1(i) + half * 128, 128)

    def send_far(j):
        src, land = o_v.at[j], r1_v.at[j]
        send(src.at[part(i1 + 2, 0)], land.at[0], "ring", ("far", j), (right1, mp))
        send(src.at[part(i1 + 2, 1)], land.at[1], "ring", ("far", j), (left1, mp))

    def far(j):
        recv(("pair", j), pr_v.at[j])
        for t in (2, 1, 3, 0):
            block = rows(quarter1(i1 + t), 256)
            o_v[j, block] += pr_v[j, block]
            if t == 2:
                send_far(j)

    def direct(j):
        src, land = o_v.at[j], r1_v.at[j]
        send(src.at[part(i1 + 1, 1)], land.at[2], "ring", ("near", j), (right1, mp))
        send(src.at[part(i1 + 3, 0)], land.at[3], "ring", ("near", j), (left1, mp))

    def aggregate(j):
        src, land = o_v.at[j], r1_v.at[j]
        recv(("far", j), land.at[0:2])
        src[part(i1 + 1, 0), :] += land[0]
        send(src.at[part(i1 + 1, 0)], land.at[4], "ring", ("near", j), (right1, mp))
        src[part(i1 + 3, 1), :] += land[1]
        send(src.at[part(i1 + 3, 1)], land.at[5], "ring", ("near", j), (left1, mp))

    def finish(j):
        src, land, dst = o_v.at[j], r1_v.at[j], t1_v.at[j]
        recv(("near", j), land.at[2:6])
        dst[0:128, :] = src[part(i1, 0), :] + land[3] + land[4]
        dst[128:256, :] = src[part(i1, 1), :] + land[2] + land[5]
        for n, (di, dz) in enumerate(EIGHT):
            block = rows(((i2 + di) % 4) * 64 + ((z + dz) % 2) * 32, 32)
            send(dst.at[block], r2_v.at[j, n], "eight", ("eight", j), (eight(di, dz), mp))

    def total(j):
        recv(("eight", j), r2_v.at[j])
        value = t1_v[j, rows(i2 * 64 + z * 32, 32)]
        for n in range(len(EIGHT)):
            value += r2_v[j, n]
        mine = cf_v.at[NC * c + j, rows(i1 * 256 + i2 * 64 + z * 32, 32)]
        mine[...] = value.astype(BF16)
        for di, dz in EIGHT:
            send(mine, mine, ("all8", j), ("all8", j), (eight(di, dz), mp))

    def to_core(j, i):
        block = cf_v.at[NC * c + j, rows(quarter1(i), 256)]
        send(block, block, ("core", j), ("core", j), (other_core, mp))

    def gather(j):
        buf = cf_v.at[NC * c + j]
        recv(("all8", j), buf.at[rows(quarter1(i1), 224)])
        block = buf.at[rows(quarter1(i1), 256)]
        for device in (right1, left1, opposite1):
            send(block, block, ("ring4", j), ("ring4", j), (device, mp))
        to_core(j, i1)

    def end(j):
        recv(("ring4", j), cf_v.at[NC * c + j, 0:768])
        for t in (1, 3, 2):
            to_core(j, i1 + t)

    def products(j):
        recv(("core", j), cf_v.at[NC * (1 - c) + j])

        def left_one(n, carry):
            k = NC * n + j
            lacc_v[...] += lax.dot_general(
                cf_v[k, rows(dp * 16, 16)], cf_v[k], (((1,), (1,)), ((), ())), preferred_element_type=F32
            )
            return carry

        def rotated_one(n, carry):
            k = NC * n + j
            lhs = jnp.concatenate(
                [cf_v[k, rows(256 * xx + 128 * z + 32 * yy + 16 * c, 16)] for xx in range(4) for yy in range(4)], 0
            )
            rhs = jnp.concatenate(
                [bp_v[2 * (k % 2) + cc, rows((4 * (k // 2) + yy) * 32, 32)] for yy in range(4) for cc in range(2)], 0
            )
            racc_v[...] += jnp.dot(lhs, rhs, preferred_element_type=F32)
            return carry

        lax.fori_loop(0, 2, left_one, 0)
        if j == NC - 1:
            lr_v[mp] = lacc_v[...].astype(BF16)
            for d in range(1, 4):
                send(lr_v.at[mp], lr_v.at[mp], "left", "left", (dp, (mp + d) % 4))
        lax.fori_loop(0, 2, rotated_one, 0)

    steps = {
        "partner": partner, "own": own, "far": far, "direct": direct, "aggregate": aggregate, "finish": finish,
        "total": total, "gather": gather, "end": end, "products": products,
        "basis_gather": lambda j: basis_gather(), "basis_forward": lambda j: basis_forward(),
        "basis_end": lambda j: basis_end(),
    }

    first_chunk()
    lacc_v[...] = jnp.zeros_like(lacc_v)
    racc_v[...] = jnp.zeros_like(racc_v)
    for step, j in ORDER:
        with jax.named_scope(f"{step}_{j}"):
            steps[step](j)

    with jax.named_scope("rotated_send"):
        rsend_v[...] = racc_v[...].astype(BF16)
        mine = rows(p_me * 128, 128, 128)
        for dx, dy in PLANE:
            p_to = 4 * ((x + dx) % 4) + (y + dy) % 4
            send(rsend_v.at[rows(p_to * 16, 16)], rot_out.at[:, mine], "rotated", "rotated", (plane(dx, dy), mp))
        rot_out[:, mine] = rsend_v[rows(p_me * 16, 16), :]

    with jax.named_scope("right"):
        ct_v[...] = cf_v[dp // 8, :, rows(128 * ((dp // 4) % 2), 128, 128)].T
        loads["right"].wait()

        def right_step(k, carry):
            cols = rows(k * 256, 256, 256)
            gram = jnp.dot(ct_v[rows(32 * (dp % 4), 32), :], cf_v[k], preferred_element_type=F32)
            right_out[0, :, cols] = 0.9 * right_v[:, cols] + 0.1 * (gram / ROWS)
            return carry

        lax.fori_loop(0, 2 * NC, right_step, 0)

    with jax.named_scope("rotated_recv"):
        recv("rotated", rsend_v.at[0:240])
    with jax.named_scope("left_recv"):
        loads["left"].wait()
        recv("left", lr_v.at[0:3])
        gram = lr_v[0].astype(F32) + lr_v[1].astype(F32) + lr_v[2].astype(F32) + lr_v[3].astype(F32)
        left_out[...] = 0.9 * left_v[...] + 0.1 * (gram / (4 * COLS))
    with jax.named_scope("sent"):
        wait_sent("pair", p_v)
        wait_sent("ring", r1_v)
        wait_sent("eight", r2_v)
        for j in range(NC):
            wait_sent(("all8", j), cf_v.at[0, 0:224])
            wait_sent(("ring4", j), cf_v.at[0, 0:768])
            wait_sent(("core", j), cf_v.at[0])
        wait_sent("basis", bp_v.at[0, 0:480])
        for name in ("basis_core", "basis_z", "basis_forward"):
            wait_sent(name, bp_v.at[0])
        wait_sent("rotated", rsend_v.at[0:240])
        wait_sent("left", lr_v.at[0:3])


def body(attn_out, out_grad, left_old, right_old, basis):
    vmem = pl.BlockSpec(memory_space=pltpu.VMEM)
    hbm = pl.BlockSpec(memory_space=pltpu.HBM)
    v = pltpu.VMEM
    args = [pltpu.with_memory_space_constraint(a, pltpu.HBM) for a in (attn_out, out_grad, left_old, right_old, basis)]
    shapes = (
        jax.ShapeDtypeStruct((16, ROWS), F32),
        jax.ShapeDtypeStruct((1, 32, COLS), F32),
        jax.ShapeDtypeStruct((16, COLS), BF16),
    )
    return pl.pallas_call(
        kernel,
        out_shape=shapes,
        in_specs=[hbm] * 5,
        out_specs=(vmem, vmem, vmem),
        scratch_shapes=[
            v((TOK, ROWS), BF16),
            v((2 * NC, TOK, W), BF16),
            v((NC, ROWS, W), F32),
            v((NC, ROWS, W), F32),
            v((NC, ROWS, W), F32),
            v((NC, 6, 128, W), F32),
            v((NC, 256, W), F32),
            v((NC, 7, 32, W), F32),
            v((2 * NC, ROWS, W), BF16),
            v((32, COLS), BF16),
            v((4, 512, 128), BF16),
            v((16, ROWS), F32),
            v((32, COLS), F32),
            v((16, ROWS), F32),
            v((4, 16, ROWS), BF16),
            v((256, 128), F32),
            v((256, 128), BF16),
            v((128, ROWS), BF16),
            pltpu.SemaphoreType.DMA((21,)),
            pltpu.SemaphoreType.DMA((36,)),
            pltpu.SemaphoreType.DMA((13,)),
        ],
        compiler_params=pltpu.CompilerParams(
            collective_id=0, has_side_effects=True, vmem_limit_bytes=48 * 1024 * 1024,
        ),
        cost_estimate=pl.CostEstimate(flops=5 * 10**9, bytes_accessed=7 * 2**20, transcendentals=0),
    )(*args)


def solution(mesh):
    return jax.shard_map(
        body,
        mesh=mesh,
        in_specs=(
            P("dp", None),
            P("dp", "mp"),
            P("dp", None),
            P("mp", "dp", None),
            P("mp", "dp", None),
        ),
        out_specs=(P("dp", None), P("mp", "dp", None), P("dp", "mp")),
        check_vma=False,
    )
```

```python
import jax
import jax.numpy as jnp
from jax import lax
from jax.experimental import pallas as pl
from jax.experimental.pallas import tpu as pltpu
from jax.sharding import PartitionSpec as P

MESH = pl.DeviceIdType.MESH
F32 = jnp.float32
BF16 = jnp.bfloat16

ROWS = 1024
TOK = 1024
COLS = 2048
HALF = 1024

CHUNKS = [(0, 256, False), (256, 256, False), (512, 128, False), (640, 128, False), (768, 128, True), (896, 128, True)]
TOGETHER = {0: (0,), 1: (1,), 2: (2, 3), 4: (4, 5)}
SEND_SEMS, RECV_SEMS, LOAD_SEMS = 42, 53, 13

PLANE = [(dx, dy) for dx in range(4) for dy in range(4) if (dx, dy) != (0, 0)]
EIGHT = [(di, dz) for di in range(4) for dz in range(2) if (di, dz) != (0, 0)]

ORDER = [
    ("partner", 2), ("own", 2), ("partner", 1), ("aggregate", 0), ("partner", 4), ("far", 2), ("direct", 2),
    ("own", 4), ("far", 3), ("direct", 3), ("finish", 0), ("basis_gather", 0), ("own", 1), ("far", 1),
    ("aggregate", 3), ("direct", 1), ("far", 5), ("aggregate", 2), ("aggregate", 1), ("far", 4), ("direct", 5),
    ("finish", 3), ("total", 0), ("aggregate", 5), ("finish", 2), ("finish", 1), ("direct", 4), ("aggregate", 4),
    ("basis_forward", 0), ("total", 3), ("finish", 5), ("total", 2), ("total", 1), ("gather", 0), ("finish", 4),
    ("total", 5), ("gather", 3), ("gather", 2), ("gather", 1), ("total", 4), ("forward", 0), ("forward", 3),
    ("gather", 5), ("forward", 2), ("forward", 1), ("gather", 4), ("end", 0), ("end", 3), ("end", 2), ("end", 5),
    ("basis_end", 0), ("products", 3), ("end", 1), ("products", 0), ("end", 4), ("products", 2), ("products", 5),
    ("products", 1), ("products", 4),
]


def rows(start, size, unit=16):
    return pl.ds(pl.multiple_of(start, unit), size)


def kernel(
    a_hbm, g_hbm, left_hbm, right_hbm, basis_hbm, left_out, right_out, rot_out,
    a_v, g_v, p_v, pr_v, o_v, r1_v, t1_v, r2_v, cf_v,
    basis_v, bp_v, left_v, right_v, lacc_v, lr_v, racc_v, rsend_v, ct_v,
    ssem, rsem, lsem,
):
    dp = lax.axis_index("dp")
    mp = lax.axis_index("mp")
    x, z, y, c = dp // 16, (dp // 8) % 2, (dp // 2) % 4, dp % 2
    i1 = x * (1 - c) + y * c
    i2 = y * (1 - c) + x * c
    s1 = 16 * (1 - c) + 2 * c
    s2 = 2 * (1 - c) + 16 * c
    right1 = dp + ((i1 + 1) % 4 - i1) * s1
    left1 = dp + ((i1 + 3) % 4 - i1) * s1
    opposite1 = dp + ((i1 + 2) % 4 - i1) * s1
    other_core = dp + 1 - 2 * c
    other_z = dp + (1 - 2 * z) * 8

    def plane(dx, dy):
        return ((x + dx) % 4) * 16 + z * 8 + ((y + dy) % 4) * 2 + c

    def eight(di, dz):
        return dp + ((i2 + di) % 4 - i2) * s2 + ((z + dz) % 2 - z) * 8

    loads = {}

    def load(name, src, dst):
        copy = pltpu.make_async_copy(src, dst, lsem.at[len(loads)])
        copy.start()
        loads[name] = copy

    def g_load(own, head):
        half = c if own else 1 - c
        load(
            ("g", own, head),
            g_hbm.at[:, rows(half * HALF + CHUNKS[head][0], 256, 128)],
            g_v[2 * list(TOGETHER).index(head) + own],
        )

    def a_load(n):
        cols = rows(((first_half + n) % 2) * 512, 512, 512)
        load(("a", n), a_hbm.at[:, cols], a_v.at[:, cols])

    first_half = ((i2 + 2) % 4) // 2
    a_load(0)
    g_load(False, 0)
    a_load(1)
    g_load(True, 0)
    load("basis", basis_hbm.at[0], basis_v)

    barrier = pltpu.get_barrier_semaphore()
    greeted = [(plane(dx, dy), mp) for dx, dy in PLANE] + [(eight(di, 1), mp) for di in range(4)]
    greeted += [(other_core, mp)] + [(dp, (mp + d) % 4) for d in range(1, 4)]
    for device in greeted:
        pl.semaphore_signal(barrier, inc=1, device_id=device, device_id_type=MESH)

    def later_loads():
        for head in list(TOGETHER)[1:]:
            g_load(False, head)
            g_load(True, head)
        load("left", left_hbm, left_v)
        load("right", right_hbm.at[0], right_v)

    sent, landed = {}, {}

    def descriptor(src, dst, out, into, device):
        return pltpu.make_async_remote_copy(
            src_ref=src, dst_ref=dst,
            send_sem=ssem.at[sent.setdefault(out, len(sent))],
            recv_sem=rsem.at[landed.setdefault(into, len(landed))],
            device_id=device, device_id_type=MESH,
        )

    def send(src, dst, out, into, device):
        descriptor(src, dst, out, into, device).start()

    def recv(into, span):
        pltpu.make_async_copy(span, span, rsem.at[landed[into]]).wait()

    def wait_sent(out, span):
        pltpu.make_async_copy(span, span, ssem.at[sent[out]]).wait()

    p_me = 4 * x + y
    zc = 2 * z + c

    def basis_begin():
        loads["basis"].wait()
        for dx, dy in PLANE:
            p_to = 4 * ((x + dx) % 4) + (y + dy) % 4
            send(
                basis_v.at[:, rows(p_to * 128, 128, 128)], bp_v.at[zc, rows(p_me * 32, 32)],
                "basis", "basis", (plane(dx, dy), mp),
            )
        bp_v[zc, rows(p_me * 32, 32)] = basis_v[:, rows(p_me * 128, 128, 128)]

    def basis_gather():
        recv("basis", bp_v.at[zc, 0:480])
        send(bp_v.at[zc], bp_v.at[zc], "basis_core", "basis_core", (other_core, mp))
        send(bp_v.at[zc], bp_v.at[zc], "basis_z", "basis_z", (other_z, mp))

    def basis_forward():
        from_z = 2 * (1 - z) + c
        recv("basis_z", bp_v.at[from_z])
        send(bp_v.at[from_z], bp_v.at[from_z], "basis_forward", "basis_forward", (other_core, mp))

    def basis_end():
        recv("basis_core", bp_v.at[2 * z + 1 - c])
        recv("basis_forward", bp_v.at[2 * (1 - z) + 1 - c])

    def quarter1(i):
        return (i % 4) * 256

    def product(refs, own, head, half):
        block = rows(half * 512, 512, 512)
        value = lax.dot_general(
            a_v[:, block], g_v[2 * list(TOGETHER).index(head) + own][...], (((0,), (0,)), ((), ())),
            preferred_element_type=F32,
        )
        for j in TOGETHER[head]:
            start = CHUNKS[j][0] - CHUNKS[head][0]
            refs[j][block, :] = value[:, start:start + CHUNKS[j][1]]

    def both_halves(refs, own, head):
        loads[("g", own, head)].wait()

        def one(half, carry):
            product(refs, own, head, half)
            return carry

        lax.fori_loop(0, 2, one, 0)

    def partner(head):
        both_halves(p_v, False, head)
        for j in TOGETHER[head]:
            send(p_v[j], pr_v[j], ("pair", j), ("pair", j), (other_core, mp))

    def own(head):
        both_halves(o_v, True, head)

    def first_chunk():
        p, o = p_v[0], o_v[0]
        my_half = ((i1 + 2) % 4) // 2
        for n in range(2):
            half = (first_half + n) % 2
            loads[("a", n)].wait()
            if n == 0:
                loads[("g", False, 0)].wait()
            with jax.named_scope("first"):
                product(p_v, False, 0, half)
            if n == 0:
                with jax.named_scope("barrier"):
                    pl.semaphore_wait(barrier, len(greeted))
            block = rows(half * 512, 512, 512)
            send(p.at[block], pr_v[0].at[block], ("pair", 0), ("pair", 0, n), (other_core, mp))
        basis_begin()
        later_loads()
        loads[("g", True, 0)].wait()
        for n in range(2):
            half = (my_half + n) % 2
            with jax.named_scope("first"):
                product(o_v, True, 0, half)
            block = rows(half * 512, 512, 512)
            recv(("pair", 0, n), pr_v[0].at[block])
            o[block, :] += pr_v[0][block, :]
            if n == 0:
                send_far(0)
        direct(0)

    def part(i, half):
        return rows(quarter1(i) + half * 128, 128)

    def send_far(j):
        src, land = o_v[j], r1_v[j]
        send(src.at[part(i1 + 2, 0)], land.at[0], ("ring", j), ("far", j), (right1, mp))
        send(src.at[part(i1 + 2, 1)], land.at[1], ("ring", j), ("far", j), (left1, mp))

    def far(j):
        recv(("pair", j), pr_v[j])
        for t in (2, 1, 3, 0):
            block = rows(quarter1(i1 + t), 256)
            o_v[j][block, :] += pr_v[j][block, :]
            if t == 2:
                send_far(j)

    def direct(j):
        src, land = o_v[j], r1_v[j]
        send(src.at[part(i1 + 1, 1)], land.at[2], ("ring", j), ("near", j), (right1, mp))
        send(src.at[part(i1 + 3, 0)], land.at[3], ("ring", j), ("near", j), (left1, mp))

    def aggregate(j):
        src, land = o_v[j], r1_v[j]
        recv(("far", j), land.at[0:2])
        src[part(i1 + 1, 0), :] += land[0]
        send(src.at[part(i1 + 1, 0)], land.at[4], ("ring", j), ("near", j), (right1, mp))
        src[part(i1 + 3, 1), :] += land[1]
        send(src.at[part(i1 + 3, 1)], land.at[5], ("ring", j), ("near", j), (left1, mp))

    def finish(j):
        src, land, dst = o_v[j], r1_v[j], t1_v[j]
        recv(("near", j), land.at[2:6])
        dst[0:128, :] = src[part(i1, 0), :] + land[3] + land[4]
        dst[128:256, :] = src[part(i1, 1), :] + land[2] + land[5]
        for n, (di, dz) in enumerate(EIGHT):
            block = rows(((i2 + di) % 4) * 64 + ((z + dz) % 2) * 32, 32)
            send(dst.at[block], r2_v[j].at[n], ("eight", j), ("eight", j), (eight(di, dz), mp))

    def total(j):
        recv(("eight", j), r2_v[j])
        value = t1_v[j][rows(i2 * 64 + z * 32, 32), :]
        for n in range(len(EIGHT)):
            value += r2_v[j][n]
        mine = cf_v[j].at[c, rows(i1 * 256 + i2 * 64 + z * 32, 32)]
        mine[...] = value.astype(BF16)
        for di, dz in EIGHT:
            send(mine, mine, ("all8", j), ("all8", j), (eight(di, dz), mp))

    def to_core(j, i):
        block = cf_v[j].at[c, rows(quarter1(i), 256)]
        send(block, block, ("core", j), ("core", j), (other_core, mp))

    def gather(j):
        buf = cf_v[j].at[c]
        recv(("all8", j), buf.at[rows(quarter1(i1), 224)])
        block = buf.at[rows(quarter1(i1), 256)]
        for device in (right1, left1) + ((opposite1,) if CHUNKS[j][2] else ()):
            send(block, block, ("four", j), ("begin", j), (device, mp))
        to_core(j, i1)

    def forward(j):
        buf = cf_v[j].at[c]
        recv(("begin", j), buf.at[0:512])
        half = buf.at[part(i1 + 3, 0)]
        send(half, half, ("four", j), ("forward", j), (right1, mp))
        half = buf.at[part(i1 + 1, 1)]
        send(half, half, ("four", j), ("forward", j), (left1, mp))
        to_core(j, i1 + 3)
        to_core(j, i1 + 1)

    def end(j):
        buf = cf_v[j].at[c]
        if CHUNKS[j][2]:
            recv(("begin", j), buf.at[0:768])
            to_core(j, i1 + 3)
            to_core(j, i1 + 1)
        else:
            recv(("forward", j), buf.at[0:256])
        to_core(j, i1 + 2)

    done = []

    def products(j):
        start, width, _ = CHUNKS[j]
        cf = cf_v[j]
        recv(("core", j), cf.at[1 - c])
        done.append(j)

        def left_one(n):
            return lax.dot_general(
                cf[n, rows(dp * 16, 16)], cf[n], (((1,), (1,)), ((), ())), preferred_element_type=F32
            )

        def rotated_one(n):
            lhs = jnp.concatenate(
                [cf[n, rows(256 * xx + 128 * z + 32 * yy + 16 * c, 16)] for xx in range(4) for yy in range(4)], 0
            )
            holders = [32 * n + start // 32 + b for b in range(width // 32)]
            rhs = jnp.concatenate(
                [bp_v[2 * ((h // 8) % 2) + h % 2, rows((4 * (h // 16) + (h // 2) % 4) * 32, 32)] for h in holders], 0
            )
            return jnp.dot(lhs, rhs, preferred_element_type=F32)

        lacc_v[...] += left_one(0) + left_one(1)
        if len(done) == len(CHUNKS):
            lr_v[mp] = lacc_v[...].astype(BF16)
            for d in range(1, 4):
                send(lr_v.at[mp], lr_v.at[mp], "left", "left", (dp, (mp + d) % 4))
        racc_v[...] += rotated_one(0) + rotated_one(1)

    steps = {
        "partner": partner, "own": own, "far": far, "direct": direct, "aggregate": aggregate, "finish": finish,
        "total": total, "gather": gather, "forward": forward, "end": end, "products": products,
        "basis_gather": lambda j: basis_gather(), "basis_forward": lambda j: basis_forward(),
        "basis_end": lambda j: basis_end(),
    }

    first_chunk()
    lacc_v[...] = jnp.zeros_like(lacc_v)
    racc_v[...] = jnp.zeros_like(racc_v)
    for step, j in ORDER:
        with jax.named_scope(f"{step}_{j}"):
            steps[step](j)

    with jax.named_scope("rotated_send"):
        rsend_v[...] = racc_v[...].astype(BF16)
        mine = rows(p_me * 128, 128, 128)
        for dx, dy in PLANE:
            p_to = 4 * ((x + dx) % 4) + (y + dy) % 4
            send(rsend_v.at[rows(p_to * 16, 16)], rot_out.at[:, mine], "rotated", "rotated", (plane(dx, dy), mp))
        rot_out[:, mine] = rsend_v[rows(p_me * 16, 16), :]

    with jax.named_scope("right"):
        column = 32 * (dp % 32)
        for j, (start, width, _) in enumerate(CHUNKS):
            @pl.when((column >= start) & (column < start + width))
            def _():
                ct_v[...] = cf_v[j][dp // 32, :, rows(((column - start) // 128) * 128, 128, 128)].T
        loads["right"].wait()
        for j, (start, width, _) in enumerate(CHUNKS):
            for n in range(2):
                cols = rows(n * HALF + start, width, 128)
                gram = jnp.dot(ct_v[rows(32 * (dp % 4), 32), :], cf_v[j][n], preferred_element_type=F32)
                right_out[0, :, cols] = 0.9 * right_v[:, cols] + 0.1 * (gram / ROWS)

    with jax.named_scope("rotated_recv"):
        recv("rotated", rsend_v.at[0:240])
    with jax.named_scope("left_recv"):
        loads["left"].wait()
        recv("left", lr_v.at[0:3])
        gram = lr_v[0].astype(F32) + lr_v[1].astype(F32) + lr_v[2].astype(F32) + lr_v[3].astype(F32)
        left_out[...] = 0.9 * left_v[...] + 0.1 * (gram / (4 * COLS))
    with jax.named_scope("sent"):
        for j in range(len(CHUNKS)):
            wait_sent(("pair", j), p_v[j])
            wait_sent(("ring", j), r1_v[j])
            wait_sent(("eight", j), r2_v[j])
            wait_sent(("all8", j), cf_v[j].at[0, 0:224])
            wait_sent(("four", j), cf_v[j].at[0, 0:768])
            wait_sent(("core", j), cf_v[j].at[0])
        wait_sent("basis", bp_v.at[0, 0:480])
        for name in ("basis_core", "basis_z", "basis_forward"):
            wait_sent(name, bp_v.at[0])
        wait_sent("rotated", rsend_v.at[0:240])
        wait_sent("left", lr_v.at[0:3])


def write_out(*refs):
    sources, results, sems = refs[:3], refs[3:6], refs[6]
    copies = [pltpu.make_async_copy(a, b, sems.at[n]) for n, (a, b) in enumerate(zip(sources, results))]
    for copy in copies:
        copy.start()
    for copy in copies:
        copy.wait()


def body(attn_out, out_grad, left_old, right_old, basis):
    vmem = pl.BlockSpec(memory_space=pltpu.VMEM)
    hbm = pl.BlockSpec(memory_space=pltpu.HBM)
    v = pltpu.VMEM
    args = [pltpu.with_memory_space_constraint(a, pltpu.HBM) for a in (attn_out, out_grad, left_old, right_old, basis)]
    shapes = (
        jax.ShapeDtypeStruct((16, ROWS), F32),
        jax.ShapeDtypeStruct((1, 32, COLS), F32),
        jax.ShapeDtypeStruct((16, COLS), BF16),
    )
    shapes = (
        jax.ShapeDtypeStruct((16, ROWS), F32),
        jax.ShapeDtypeStruct((1, 32, COLS), F32),
        jax.ShapeDtypeStruct((16, COLS), BF16),
    )
    results = pl.pallas_call(
        kernel,
        out_shape=tuple(pltpu.VMEM(q.shape, q.dtype) for q in shapes),
        in_specs=[hbm] * 5,
        out_specs=(vmem, vmem, vmem),
        scratch_shapes=[
            v((TOK, ROWS), BF16),
            [v((TOK, 256), BF16) for _ in range(2 * len(TOGETHER))],
            [v((ROWS, w), F32) for _, w, _ in CHUNKS],
            [v((ROWS, w), F32) for _, w, _ in CHUNKS],
            [v((ROWS, w), F32) for _, w, _ in CHUNKS],
            [v((6, 128, w), F32) for _, w, _ in CHUNKS],
            [v((256, w), F32) for _, w, _ in CHUNKS],
            [v((7, 32, w), F32) for _, w, _ in CHUNKS],
            [v((2, ROWS, w), BF16) for _, w, _ in CHUNKS],
            v((32, COLS), BF16),
            v((4, 512, 128), BF16),
            v((16, ROWS), F32),
            v((32, COLS), F32),
            v((16, ROWS), F32),
            v((4, 16, ROWS), BF16),
            v((256, 128), F32),
            v((256, 128), BF16),
            v((128, ROWS), BF16),
            pltpu.SemaphoreType.DMA((SEND_SEMS,)),
            pltpu.SemaphoreType.DMA((RECV_SEMS,)),
            pltpu.SemaphoreType.DMA((LOAD_SEMS,)),
        ],
        compiler_params=pltpu.CompilerParams(
            collective_id=0, has_side_effects=True, vmem_limit_bytes=48 * 1024 * 1024,
        ),
        cost_estimate=pl.CostEstimate(flops=5 * 10**9, bytes_accessed=7 * 2**20, transcendentals=0),
    )(*args)
    return pl.pallas_call(
        write_out,
        out_shape=shapes,
        in_specs=[vmem] * 3,
        out_specs=(hbm,) * 3,
        scratch_shapes=[pltpu.SemaphoreType.DMA((3,))],
    )(*(pltpu.with_memory_space_constraint(r, pltpu.VMEM) for r in results))


def solution(mesh):
    return jax.shard_map(
        body,
        mesh=mesh,
        in_specs=(
            P("dp", None),
            P("dp", "mp"),
            P("dp", None),
            P("mp", "dp", None),
            P("mp", "dp", None),
        ),
        out_specs=(P("dp", None), P("mp", "dp", None), P("dp", "mp")),
        check_vma=False,
    )
```

```python
import jax
import jax.numpy as jnp
from jax import lax
from jax.experimental import pallas as pl
from jax.experimental.pallas import tpu as pltpu
from jax.sharding import PartitionSpec as P

MESH = pl.DeviceIdType.MESH
F32 = jnp.float32
BF16 = jnp.bfloat16

ROWS = 1024
TOK = 1024
COLS = 2048
HALF = 1024

CHUNKS = [(0, 256, False), (256, 256, False), (512, 128, True), (640, 128, True), (768, 128, False), (896, 128, False)]
TOGETHER = {0: (0,), 1: (1,), 2: (2, 3), 4: (4, 5)}
SEND_SEMS, RECV_SEMS, LOAD_SEMS = 14, 53, 13

PLANE = [(dx, dy) for dx in range(4) for dy in range(4) if (dx, dy) != (0, 0)]
EIGHT = [(di, dz) for di in range(4) for dz in range(2) if (di, dz) != (0, 0)]

ORDER = [
    ("partner", 4), ("own", 4), ("partner", 1), ("aggregate", 0), ("partner", 2), ("far", 4), ("far", 5),
    ("direct", 5), ("direct", 4), ("own", 1), ("far", 1), ("finish", 0), ("basis_gather", 0), ("aggregate", 5),
    ("direct", 1), ("own", 2), ("aggregate", 1), ("total", 0), ("far", 2), ("finish", 5), ("far", 3),
    ("aggregate", 4), ("finish", 1), ("direct", 2), ("aggregate", 2), ("direct", 3), ("aggregate", 3),
    ("basis_forward", 0), ("finish", 4), ("total", 1), ("total", 5), ("gather", 0), ("finish", 3), ("total", 4),
    ("finish", 2), ("gather", 1), ("gather", 5), ("total", 3), ("forward", 0), ("gather", 4), ("total", 2),
    ("forward", 1), ("forward", 5), ("gather", 3), ("forward", 4), ("gather", 2), ("end", 0), ("end", 1), ("end", 5),
    ("end", 3), ("end", 4), ("basis_end", 0), ("products", 1), ("end", 2), ("products", 0), ("products", 5),
    ("products", 4), ("products", 3), ("products", 2),
]


def rows(start, size, unit=16):
    return pl.ds(pl.multiple_of(start, unit), size)


def kernel(
    a_hbm, g_hbm, left_hbm, right_hbm, basis_hbm, left_out, right_out, rot_out,
    a_v, g_v, p_v, pr_v, o_v, r1_v, t1_v, r2_v, cf_v,
    basis_v, bp_v, left_v, right_v, lacc_v, lr_v, racc_v, rsend_v, ct_v,
    ssem, rsem, lsem,
):
    dp = lax.axis_index("dp")
    mp = lax.axis_index("mp")
    x, z, y, c = dp // 16, (dp // 8) % 2, (dp // 2) % 4, dp % 2
    i1 = x * (1 - c) + y * c
    i2 = y * (1 - c) + x * c
    s1 = 16 * (1 - c) + 2 * c
    s2 = 2 * (1 - c) + 16 * c
    right1 = dp + ((i1 + 1) % 4 - i1) * s1
    left1 = dp + ((i1 + 3) % 4 - i1) * s1
    opposite1 = dp + ((i1 + 2) % 4 - i1) * s1
    other_core = dp + 1 - 2 * c
    other_z = dp + (1 - 2 * z) * 8

    def plane(dx, dy):
        return ((x + dx) % 4) * 16 + z * 8 + ((y + dy) % 4) * 2 + c

    def eight(di, dz):
        return dp + ((i2 + di) % 4 - i2) * s2 + ((z + dz) % 2 - z) * 8

    loads = {}

    def load(name, src, dst):
        copy = pltpu.make_async_copy(src, dst, lsem.at[len(loads)])
        copy.start()
        loads[name] = copy

    def g_load(own, head):
        half = c if own else 1 - c
        load(
            ("g", own, head),
            g_hbm.at[:, rows(half * HALF + CHUNKS[head][0], 256, 128)],
            g_v[2 * list(TOGETHER).index(head) + own],
        )

    def a_load(n):
        cols = rows(((first_half + n) % 2) * 512, 512, 512)
        load(("a", n), a_hbm.at[:, cols], a_v.at[:, cols])

    first_half = ((i2 + 2) % 4) // 2
    a_load(0)
    g_load(False, 0)
    a_load(1)
    g_load(True, 0)
    load("basis", basis_hbm.at[0], basis_v)

    barrier = pltpu.get_barrier_semaphore()
    greeted = [(plane(dx, dy), mp) for dx, dy in PLANE] + [(eight(di, 1), mp) for di in range(4)]
    greeted += [(other_core, mp)] + [(dp, (mp + d) % 4) for d in range(1, 4)]
    for device in greeted:
        pl.semaphore_signal(barrier, inc=1, device_id=device, device_id_type=MESH)

    def later_loads():
        for head in list(TOGETHER)[1:]:
            g_load(False, head)
            g_load(True, head)
        load("left", left_hbm, left_v)
        load("right", right_hbm.at[0], right_v)

    sent, landed = {}, {}

    def descriptor(src, dst, out, into, device):
        return pltpu.make_async_remote_copy(
            src_ref=src, dst_ref=dst,
            send_sem=ssem.at[sent.setdefault(out, len(sent))],
            recv_sem=rsem.at[landed.setdefault(into, len(landed))],
            device_id=device, device_id_type=MESH,
        )

    def send(src, dst, out, into, device):
        descriptor(src, dst, out, into, device).start()

    def recv(into, span):
        pltpu.make_async_copy(span, span, rsem.at[landed[into]]).wait()

    def wait_sent(out, span):
        pltpu.make_async_copy(span, span, ssem.at[sent[out]]).wait()

    p_me = 4 * x + y
    zc = 2 * z + c

    def basis_begin():
        loads["basis"].wait()
        for dx, dy in PLANE:
            p_to = 4 * ((x + dx) % 4) + (y + dy) % 4
            send(
                basis_v.at[:, rows(p_to * 128, 128, 128)], bp_v.at[zc, rows(p_me * 32, 32)],
                "basis", "basis", (plane(dx, dy), mp),
            )
        bp_v[zc, rows(p_me * 32, 32)] = basis_v[:, rows(p_me * 128, 128, 128)]

    def basis_gather():
        recv("basis", bp_v.at[zc, 0:480])
        send(bp_v.at[zc], bp_v.at[zc], "basis_core", "basis_core", (other_core, mp))
        send(bp_v.at[zc], bp_v.at[zc], "basis_z", "basis_z", (other_z, mp))

    def basis_forward():
        from_z = 2 * (1 - z) + c
        recv("basis_z", bp_v.at[from_z])
        send(bp_v.at[from_z], bp_v.at[from_z], "basis_forward", "basis_forward", (other_core, mp))

    def basis_end():
        recv("basis_core", bp_v.at[2 * z + 1 - c])
        recv("basis_forward", bp_v.at[2 * (1 - z) + 1 - c])

    def quarter1(i):
        return (i % 4) * 256

    def product(refs, own, head, half):
        block = rows(half * 512, 512, 512)
        value = lax.dot_general(
            a_v[:, block], g_v[2 * list(TOGETHER).index(head) + own][...], (((0,), (0,)), ((), ())),
            preferred_element_type=F32,
        )
        for j in TOGETHER[head]:
            start = CHUNKS[j][0] - CHUNKS[head][0]
            refs[j][block, :] = value[:, start:start + CHUNKS[j][1]]

    def both_halves(refs, own, head):
        loads[("g", own, head)].wait()

        def one(half, carry):
            product(refs, own, head, half)
            return carry

        lax.fori_loop(0, 2, one, 0)

    def partner(head):
        both_halves(p_v, False, head)
        for j in TOGETHER[head]:
            send(p_v[j], pr_v[j], ("pair", CHUNKS[j][0] // 512), ("pair", j), (other_core, mp))

    def own(head):
        both_halves(o_v, True, head)

    def first_chunk():
        p, o = p_v[0], o_v[0]
        my_half = ((i1 + 2) % 4) // 2
        for n in range(2):
            half = (first_half + n) % 2
            loads[("a", n)].wait()
            if n == 0:
                loads[("g", False, 0)].wait()
            with jax.named_scope("first"):
                product(p_v, False, 0, half)
            if n == 0:
                with jax.named_scope("barrier"):
                    pl.semaphore_wait(barrier, len(greeted))
            block = rows(half * 512, 512, 512)
            send(p.at[block], pr_v[0].at[block], ("pair", 0), ("pair", 0, n), (other_core, mp))
        basis_begin()
        later_loads()
        loads[("g", True, 0)].wait()
        for n in range(2):
            half = (my_half + n) % 2
            with jax.named_scope("first"):
                product(o_v, True, 0, half)
            block = rows(half * 512, 512, 512)
            recv(("pair", 0, n), pr_v[0].at[block])
            o[block, :] += pr_v[0][block, :]
            if n == 0:
                send_far(0)
        direct(0)

    def part(i, half):
        return rows(quarter1(i) + half * 128, 128)

    def send_far(j):
        src, land = o_v[j], r1_v[j]
        send(src.at[part(i1 + 2, 0)], land.at[0], ("ring", CHUNKS[j][0] // 512), ("far", j), (right1, mp))
        send(src.at[part(i1 + 2, 1)], land.at[1], ("ring", CHUNKS[j][0] // 512), ("far", j), (left1, mp))

    def far(j):
        recv(("pair", j), pr_v[j])
        for t in (2, 1, 3, 0):
            block = rows(quarter1(i1 + t), 256)
            o_v[j][block, :] += pr_v[j][block, :]
            if t == 2:
                send_far(j)

    def direct(j):
        src, land = o_v[j], r1_v[j]
        send(src.at[part(i1 + 1, 1)], land.at[2], ("ring", CHUNKS[j][0] // 512), ("near", j), (right1, mp))
        send(src.at[part(i1 + 3, 0)], land.at[3], ("ring", CHUNKS[j][0] // 512), ("near", j), (left1, mp))

    def aggregate(j):
        src, land = o_v[j], r1_v[j]
        recv(("far", j), land.at[0:2])
        src[part(i1 + 1, 0), :] += land[0]
        send(src.at[part(i1 + 1, 0)], land.at[4], ("ring", CHUNKS[j][0] // 512), ("near", j), (right1, mp))
        src[part(i1 + 3, 1), :] += land[1]
        send(src.at[part(i1 + 3, 1)], land.at[5], ("ring", CHUNKS[j][0] // 512), ("near", j), (left1, mp))

    def finish(j):
        src, land, dst = o_v[j], r1_v[j], t1_v[j]
        recv(("near", j), land.at[2:6])
        dst[0:128, :] = src[part(i1, 0), :] + land[3] + land[4]
        dst[128:256, :] = src[part(i1, 1), :] + land[2] + land[5]
        for n, (di, dz) in enumerate(EIGHT):
            block = rows(((i2 + di) % 4) * 64 + ((z + dz) % 2) * 32, 32)
            send(dst.at[block], r2_v[j].at[n], "eight", ("eight", j), (eight(di, dz), mp))

    def total(j):
        recv(("eight", j), r2_v[j])
        value = t1_v[j][rows(i2 * 64 + z * 32, 32), :]
        for n in range(len(EIGHT)):
            value += r2_v[j][n]
        mine = cf_v[j].at[c, rows(i1 * 256 + i2 * 64 + z * 32, 32)]
        mine[...] = value.astype(BF16)
        for di, dz in EIGHT:
            send(mine, mine, "all8", ("all8", j), (eight(di, dz), mp))

    def to_core(j, i):
        block = cf_v[j].at[c, rows(quarter1(i), 256)]
        send(block, block, "core", ("core", j), (other_core, mp))

    def gather(j):
        buf = cf_v[j].at[c]
        recv(("all8", j), buf.at[rows(quarter1(i1), 224)])
        block = buf.at[rows(quarter1(i1), 256)]
        for device in (right1, left1) + ((opposite1,) if CHUNKS[j][2] else ()):
            send(block, block, "four", ("begin", j), (device, mp))
        to_core(j, i1)

    def forward(j):
        buf = cf_v[j].at[c]
        recv(("begin", j), buf.at[0:512])
        half = buf.at[part(i1 + 3, 0)]
        send(half, half, "four", ("forward", j), (right1, mp))
        half = buf.at[part(i1 + 1, 1)]
        send(half, half, "four", ("forward", j), (left1, mp))
        to_core(j, i1 + 3)
        to_core(j, i1 + 1)

    def end(j):
        buf = cf_v[j].at[c]
        if CHUNKS[j][2]:
            recv(("begin", j), buf.at[0:768])
            to_core(j, i1 + 3)
            to_core(j, i1 + 1)
        else:
            recv(("forward", j), buf.at[0:256])
        to_core(j, i1 + 2)

    done = []

    def products(j):
        start, width, _ = CHUNKS[j]
        cf = cf_v[j]
        recv(("core", j), cf.at[1 - c])
        done.append(j)

        def left_one(n):
            return lax.dot_general(
                cf[n, rows(dp * 16, 16)], cf[n], (((1,), (1,)), ((), ())), preferred_element_type=F32
            )

        def rotated_one(n):
            lhs = jnp.concatenate(
                [cf[n, rows(256 * xx + 128 * z + 32 * yy + 16 * c, 16)] for xx in range(4) for yy in range(4)], 0
            )
            holders = [32 * n + start // 32 + b for b in range(width // 32)]
            rhs = jnp.concatenate(
                [bp_v[2 * ((h // 8) % 2) + h % 2, rows((4 * (h // 16) + (h // 2) % 4) * 32, 32)] for h in holders], 0
            )
            return jnp.dot(lhs, rhs, preferred_element_type=F32)

        lacc_v[...] += left_one(0) + left_one(1)
        if len(done) == len(CHUNKS):
            lr_v[mp] = lacc_v[...].astype(BF16)
            for d in range(1, 4):
                send(lr_v.at[mp], lr_v.at[mp], "left", "left", (dp, (mp + d) % 4))
        racc_v[...] += rotated_one(0) + rotated_one(1)

    steps = {
        "partner": partner, "own": own, "far": far, "direct": direct, "aggregate": aggregate, "finish": finish,
        "total": total, "gather": gather, "forward": forward, "end": end, "products": products,
        "basis_gather": lambda j: basis_gather(), "basis_forward": lambda j: basis_forward(),
        "basis_end": lambda j: basis_end(),
    }

    first_chunk()
    lacc_v[...] = jnp.zeros_like(lacc_v)
    racc_v[...] = jnp.zeros_like(racc_v)
    for step, j in ORDER:
        with jax.named_scope(f"{step}_{j}"):
            steps[step](j)

    with jax.named_scope("rotated_send"):
        rsend_v[...] = racc_v[...].astype(BF16)
        mine = rows(p_me * 128, 128, 128)
        for dx, dy in PLANE:
            p_to = 4 * ((x + dx) % 4) + (y + dy) % 4
            send(rsend_v.at[rows(p_to * 16, 16)], rot_out.at[:, mine], "rotated", "rotated", (plane(dx, dy), mp))
        rot_out[:, mine] = rsend_v[rows(p_me * 16, 16), :]

    with jax.named_scope("right"):
        column = 32 * (dp % 32)
        for j, (start, width, _) in enumerate(CHUNKS):
            @pl.when((column >= start) & (column < start + width))
            def _():
                ct_v[...] = cf_v[j][dp // 32, :, rows(((column - start) // 128) * 128, 128, 128)].T
        loads["right"].wait()
        for j, (start, width, _) in enumerate(CHUNKS):
            for n in range(2):
                cols = rows(n * HALF + start, width, 128)
                gram = jnp.dot(ct_v[rows(32 * (dp % 4), 32), :], cf_v[j][n], preferred_element_type=F32)
                right_out[0, :, cols] = 0.9 * right_v[:, cols] + 0.1 * (gram / ROWS)

    with jax.named_scope("rotated_recv"):
        recv("rotated", rsend_v.at[0:240])
    with jax.named_scope("left_recv"):
        loads["left"].wait()
        recv("left", lr_v.at[0:3])
        gram = lr_v[0].astype(F32) + lr_v[1].astype(F32) + lr_v[2].astype(F32) + lr_v[3].astype(F32)
        left_out[...] = 0.9 * left_v[...] + 0.1 * (gram / (4 * COLS))
    with jax.named_scope("sent"):
        for n in range(2):
            wait_sent(("pair", n), a_v)
            wait_sent(("ring", n), a_v.at[0:768])
        wait_sent("eight", a_v.at[0:448])
        wait_sent("all8", a_v.at[0:224])
        wait_sent("four", a_v.at[0:768])
        wait_sent("core", a_v)
        wait_sent("basis", bp_v.at[0, 0:480])
        for name in ("basis_core", "basis_z", "basis_forward"):
            wait_sent(name, bp_v.at[0])
        wait_sent("rotated", rsend_v.at[0:240])
        wait_sent("left", lr_v.at[0:3])


def write_out(*refs):
    sources, results, sems = refs[:3], refs[3:6], refs[6]
    copies = [pltpu.make_async_copy(a, b, sems.at[n]) for n, (a, b) in enumerate(zip(sources, results))]
    for copy in copies:
        copy.start()
    for copy in copies:
        copy.wait()


def body(attn_out, out_grad, left_old, right_old, basis):
    vmem = pl.BlockSpec(memory_space=pltpu.VMEM)
    hbm = pl.BlockSpec(memory_space=pltpu.HBM)
    v = pltpu.VMEM
    args = [pltpu.with_memory_space_constraint(a, pltpu.HBM) for a in (attn_out, out_grad, left_old, right_old, basis)]
    shapes = (
        jax.ShapeDtypeStruct((16, ROWS), F32),
        jax.ShapeDtypeStruct((1, 32, COLS), F32),
        jax.ShapeDtypeStruct((16, COLS), BF16),
    )
    shapes = (
        jax.ShapeDtypeStruct((16, ROWS), F32),
        jax.ShapeDtypeStruct((1, 32, COLS), F32),
        jax.ShapeDtypeStruct((16, COLS), BF16),
    )
    results = pl.pallas_call(
        kernel,
        out_shape=tuple(pltpu.VMEM(q.shape, q.dtype) for q in shapes),
        in_specs=[hbm] * 5,
        out_specs=(vmem, vmem, vmem),
        scratch_shapes=[
            v((TOK, ROWS), BF16),
            [v((TOK, 256), BF16) for _ in range(2 * len(TOGETHER))],
            [v((ROWS, w), F32) for _, w, _ in CHUNKS],
            [v((ROWS, w), F32) for _, w, _ in CHUNKS],
            [v((ROWS, w), F32) for _, w, _ in CHUNKS],
            [v((6, 128, w), F32) for _, w, _ in CHUNKS],
            [v((256, w), F32) for _, w, _ in CHUNKS],
            [v((7, 32, w), F32) for _, w, _ in CHUNKS],
            [v((2, ROWS, w), BF16) for _, w, _ in CHUNKS],
            v((32, COLS), BF16),
            v((4, 512, 128), BF16),
            v((16, ROWS), F32),
            v((32, COLS), F32),
            v((16, ROWS), F32),
            v((4, 16, ROWS), BF16),
            v((256, 128), F32),
            v((256, 128), BF16),
            v((128, ROWS), BF16),
            pltpu.SemaphoreType.DMA((SEND_SEMS,)),
            pltpu.SemaphoreType.DMA((RECV_SEMS,)),
            pltpu.SemaphoreType.DMA((LOAD_SEMS,)),
        ],
        compiler_params=pltpu.CompilerParams(
            collective_id=0, has_side_effects=True, vmem_limit_bytes=48 * 1024 * 1024,
        ),
        cost_estimate=pl.CostEstimate(flops=5 * 10**9, bytes_accessed=7 * 2**20, transcendentals=0),
    )(*args)
    return pl.pallas_call(
        write_out,
        out_shape=shapes,
        in_specs=[vmem] * 3,
        out_specs=(hbm,) * 3,
        scratch_shapes=[pltpu.SemaphoreType.DMA((3,))],
    )(*(pltpu.with_memory_space_constraint(r, pltpu.VMEM) for r in results))


def solution(mesh):
    return jax.shard_map(
        body,
        mesh=mesh,
        in_specs=(
            P("dp", None),
            P("dp", "mp"),
            P("dp", None),
            P("mp", "dp", None),
            P("mp", "dp", None),
        ),
        out_specs=(P("dp", None), P("mp", "dp", None), P("dp", "mp")),
        check_vma=False,
    )
```
